256 devices in a mesh: tm: 4 (over y), seq: 64 (over x, z, core).
Axes of the slice: x: 4, y: 4, z: 8, core: 2. Of those that a mesh axis runs over, the one named last changes fastest.
Arguments:
- queries: bfloat16 [12288, 4096], P(('tm', 'seq'))
- keys: bfloat16 [12288, 4096], P(('tm', 'seq'))
- values: bfloat16 [12288, 4096], P(('tm', 'seq')), may hold values from -6 to 6
- span_rank: int32 [4], replicated, may hold values from 0 to 3, each once
- token_counts: int32 [4], replicated, may hold values from 1536 to 3072, as said below
Outputs:
- attended: bfloat16 [12288, 4096], P(('tm', 'seq'))
The draws below stay inside these ranges and needn't reach their ends.
Inputs may be any that keep to these rules, and one draw needn't show every extreme that they name: Each span's valid tokens are its first token_counts slots; at least one span is full.
All inputs are finite; a program needn't handle non-finite values.
Results may differ from the reference program's by a relative error of at most 0.009.
Values may be sent and summed in bfloat16 or wider, within the bound.
A program may use at most 64 MiB of HBM per device.

```python
import jax
import jax.numpy as jnp
from jax import lax

HEADS = 32
HS = 128
SPAN = 3072
TOTAL = 12288
N_TM = 4


def draw_queries(key, part):
    key = jax.random.fold_in(key, 11)
    base = jax.random.normal(key, (TOTAL, HEADS * HS), jnp.float32)
    return base.astype(jnp.bfloat16)


def draw_keys(key, part):
    key = jax.random.fold_in(key, 23)
    base = jax.random.normal(key, (TOTAL, HEADS * HS), jnp.float32)
    return base.astype(jnp.bfloat16)


def draw_token_counts(key, part):
    key = jax.random.fold_in(key, 37)
    first_key, second_key = jax.random.split(key)
    counts = jax.random.randint(first_key, (N_TM,), SPAN // 2, SPAN + 1, jnp.int32)
    full_one = jax.random.randint(second_key, (), 0, N_TM, jnp.int32)
    return jnp.where(jnp.arange(N_TM, dtype=jnp.int32) == full_one, SPAN, counts).astype(jnp.int32)


def levels(own_key, extent, cuts, least, high):
    loudness = 1.0
    for axis_at, shards_of in cuts:
        draws = jax.random.uniform(jax.random.fold_in(jax.random.fold_in(own_key, 6), axis_at), (shards_of,), jnp.float32, least / len(cuts), high / len(cuts))
        loudness = loudness * jnp.repeat(jnp.exp(draws), extent[axis_at] // shards_of).reshape((-1,) + (1,) * (len(extent) - 1 - axis_at))
    return loudness


def centred(rng, shape, scale, bound, cuts=(), kind=jnp.bfloat16):
    level = levels(rng, shape, cuts, -0.22, 0.18) if cuts else 1.0
    drawn = jax.random.normal(rng, shape, jnp.float32) * scale * level
    return jnp.minimum(jnp.maximum(drawn, -bound), bound).astype(kind)


def setup_inputs(seed: int = 0) -> dict:
    splits = jax.random.split(jax.random.key(seed), 6)
    queries = draw_queries(jax.random.fold_in(splits[5], 71), 0)
    keys = draw_keys(jax.random.fold_in(splits[5], 71), 0)
    values = centred(splits[2], (TOTAL, HEADS * HS), 1.0, 6.0, ((0, 256),))
    span_rank = jax.random.permutation(splits[3], N_TM).astype(jnp.int32)
    token_counts = draw_token_counts(jax.random.fold_in(splits[5], 71), 0)
    return {"queries": queries, "keys": keys, "values": values, "span_rank": span_rank, "token_counts": token_counts}


def reference(queries, keys, values, span_rank, token_counts):
    slots = jnp.arange(TOTAL, dtype=jnp.int32)
    owner = slots // SPAN
    inside = slots % SPAN
    rank_of = span_rank[owner]
    valid = inside < token_counts[owner]
    allowed = (rank_of[None, :] <= rank_of[:, None]) & valid[None, :]
    score_scale = HS ** -0.5
    query_heads = queries.reshape(TOTAL, HEADS, HS).transpose(1, 0, 2)
    key_heads = keys.reshape(TOTAL, HEADS, HS).transpose(1, 0, 2)
    value_heads = values.reshape(TOTAL, HEADS, HS).transpose(1, 0, 2)

    def one_head(operands):
        query_one, key_one, value_one = operands
        scores = jnp.dot(query_one, key_one.T, preferred_element_type=jnp.float32) * score_scale
        scores = jnp.where(allowed, scores, -1e30)
        upper = jnp.max(scores, axis=1, keepdims=True)
        weights = jnp.where(allowed, jnp.exp(scores - upper), 0.0)
        total = jnp.sum(weights, axis=1, keepdims=True)
        accum = jnp.dot(weights.astype(jnp.bfloat16), value_one, preferred_element_type=jnp.float32)
        return (accum / total).astype(jnp.bfloat16)

    result = lax.map(one_head, (query_heads, key_heads, value_heads))
    return result.transpose(1, 0, 2).reshape(TOTAL, HEADS * HS)
```

```python
import functools

import jax
import jax.numpy as jnp
from jax import lax
from jax.experimental import pallas as pl
from jax.experimental.pallas import tpu as pltpu
from jax.sharding import PartitionSpec as P

MESH = pl.DeviceIdType.MESH
HS = 128
NX, NZ, NY = 4, 8, 4
ROWS = 48
CHUNK_DZ = ((1, 7), (2, 6), (3, 5), (0, 4))
G = len(CHUNK_DZ)
PER = 8
HALF = PER * ROWS
KEYS = 2 * HALF
NQ = 8 * ROWS
SCALE = HS ** (-0.5) * 1.4426950408889634
TK = 256
FLAG_COMPUTE = True
FLAG_Y = True
FLAG_D2D = True
FLAG_Q = True
FLAG_O = True
Q_AT = 1
ORDER_DX = (0, 1, 2, 3)


def lanesum(p):
    total = p[:, :HS]
    for at in range(HS, p.shape[1], HS):
        total = total + p[:, at : at + HS]
    return total


def kernel(rank_ref, count_ref, q_ref, k_ref, v_ref, out_ref, kv0, kv1, kv2, kv3, qb, qs, ob, os, m_s, l_s, a_s,
           a2a_sem, lr_sem, far_sem, d2d_sem, q_sem, o_sem, kv_send, q_send, o_send, y_send, f_send, d_send):
    kvb = (kv0, kv1, kv2, kv3)
    y = lax.axis_index("tm")
    s = lax.axis_index("seq")
    h = s // 2
    c = s % 2
    x = h // NZ
    z = h % NZ

    def at(dx, dy, dz):
        hd = ((x + dx) % NX) * NZ + (z + dz) % NZ
        return (y + dy) % NY, hd

    def send_kv(g):
        for i, dz in enumerate(CHUNK_DZ[g]):
            for n, dx in enumerate(ORDER_DX):
                slot = i * NX + n
                _, hd = at(dx, 0, dz)
                cols = pl.ds(pl.multiple_of(hd * HS, HS), HS)
                for j, ref in enumerate((k_ref, v_ref)):
                    src = ref.at[:, cols]
                    dst = kvb[g].at[0, j, pl.ds(slot * ROWS, ROWS), :]
                    if dx == 0 and dz == 0:
                        pltpu.make_async_copy(src, dst, a2a_sem.at[g]).start()
                    else:
                        pltpu.make_async_remote_copy(
                            src, dst, kv_send, a2a_sem.at[g], device_id=(y, 2 * hd + c), device_id_type=MESH
                        ).start()

    def send_q():
        for dz in range(NZ):
            for dx in range(NX):
                dy = dz % NY
                yd, hd = at(dx, dy, dz)
                src = q_ref.at[:, pl.ds(pl.multiple_of(hd * HS, HS), HS)]
                dst = qb.at[dy, pl.ds(((dz // NY) * NX + dx) * ROWS, ROWS), :]
                if dx == 0 and dz == 0:
                    pltpu.make_async_copy(src, dst, q_sem).start()
                else:
                    pltpu.make_async_remote_copy(
                        src, dst, q_send, q_sem, device_id=(yd, 2 * hd + c), device_id_type=MESH
                    ).start()

    def send_o(dy):
        cols = pl.ds(pl.multiple_of(h * HS, HS), HS)
        for dz in (dy, dy + NY):
            for dx in range(NX):
                yd, hd = at(-dx, -dy, -dz)
                src = ob.at[dy, pl.ds(((dz // NY) * NX + dx) * ROWS, ROWS), :]
                dst = out_ref.at[:, cols]
                if dx == 0 and dz == 0:
                    pltpu.make_async_copy(src, dst, o_sem).start()
                else:
                    pltpu.make_async_remote_copy(
                        src, dst, o_send, o_sem, device_id=(yd, 2 * hd + c), device_id_type=MESH
                    ).start()

    def wait(ref, sem):
        pltpu.make_async_copy(ref, ref, sem).wait()

    def half(g, d, j=None):
        if j is None:
            return kvb[g].at[d, :, pl.ds(0, HALF), :]
        return kvb[g].at[d, j, pl.ds(0, HALF), :]

    def other(g, d):
        return kvb[g].at[d, :, pl.ds(HALF, HALF), :]

    def y_copy(g, to_right):
        step, d = (1, 3) if to_right else (-1, 1)
        return pltpu.make_async_remote_copy(
            half(g, 0), half(g, d), y_send.at[g, int(to_right)], lr_sem.at[g, int(to_right)],
            device_id=((y + step) % NY, s), device_id_type=MESH)

    def far_copy(g, to_right):
        step, d, j = (1, 3, 0) if to_right else (-1, 1, 1)
        return pltpu.make_async_remote_copy(
            half(g, d, j), half(g, 2, j), f_send.at[g, int(to_right)], far_sem.at[g, int(to_right)],
            device_id=((y + step) % NY, s), device_id_type=MESH)

    def d2d_copy(g, d):
        return pltpu.make_async_remote_copy(
            half(g, d), other(g, d), d_send.at[g, d], d2d_sem.at[g, d],
            device_id=(y, s + 1 - 2 * c), device_id_type=MESH)

    def stage_a(g):
        wait(half(g, 0), a2a_sem.at[g])
        if FLAG_Y:
            y_copy(g, True).start()
            y_copy(g, False).start()
        if FLAG_D2D:
            d2d_copy(g, 0).start()

    def stage_b(g):
        for right in (True, False):
            if FLAG_Y:
                y_copy(g, right).wait_recv()
                far_copy(g, right).start()
            if FLAG_D2D:
                d2d_copy(g, 3 if right else 1).start()

    def stage_c(g):
        if FLAG_Y:
            far_copy(g, True).wait_recv()
            far_copy(g, False).wait_recv()
        if FLAG_D2D:
            d2d_copy(g, 2).start()

    def stage_d(g):
        if FLAG_D2D:
            for d in range(4):
                d2d_copy(g, d).wait_recv()

    ranks = [rank_ref[t] for t in range(4)]

    def order(r):
        return lax.rem(sum(jnp.where(ranks[t] == r, t, 0) for t in range(1, 4)), 4)

    def positions(g):
        col = lax.broadcasted_iota(jnp.int32, (8, KEYS), 1)
        pos = col
        for m in range(2):
            core = c if m == 0 else 1 - c
            for i, dz in enumerate(CHUNK_DZ[g]):
                for n, dx in enumerate(ORDER_DX):
                    first = m * HALF + (i * NX + n) * ROWS
                    _, hd = at(-dx, 0, -dz)
                    base = (2 * hd + core) * ROWS - first
                    pos = jnp.where((col >= first) & (col < first + ROWS), col + base, pos)
        return pos[:1]

    def compute(g):
        pos = positions(g)
        for j in range(4):
            t = order(j)
            d = lax.rem(t - y + 4, 4)
            limit = count_ref[t]
            rows = pl.ds(j * NQ, (4 - j) * NQ)
            for at_key in range(0, KEYS, TK):
                k = kvb[g][d, 0, at_key : at_key + TK, :]
                v = kvb[g][d, 1, at_key : at_key + TK, :]
                live = pos[:, at_key : at_key + TK] < limit
                scores = lax.dot_general(qs[rows, :], k, (((1,), (1,)), ((), ())), preferred_element_type=jnp.float32)
                scores = jnp.where(live, scores, -1e30)
                before = m_s[rows, :]
                upper = jnp.maximum(before, jnp.max(scores, axis=1, keepdims=True) * SCALE)
                rescale = jnp.exp2(before - upper)
                weights = jnp.exp2(scores * SCALE - jnp.concatenate([upper] * (TK // HS), axis=1))
                l_s[rows, :] = l_s[rows, :] * rescale + lanesum(weights)
                a_s[rows, :] = a_s[rows, :] * rescale + jnp.dot(
                    weights.astype(jnp.bfloat16), v, preferred_element_type=jnp.float32)
                m_s[rows, :] = upper

    for g in range(G):
        if g == Q_AT and FLAG_Q:
            send_q()
        send_kv(g)
    if Q_AT >= G and FLAG_Q:
        send_q()
    if FLAG_COMPUTE:
        m_s[...] = jnp.full(m_s.shape, -1e30, jnp.float32)
        l_s[...] = jnp.zeros(l_s.shape, jnp.float32)
        a_s[...] = jnp.zeros(a_s.shape, jnp.float32)
    for step in range(G + 3):
        if step < G:
            stage_a(step)
        if 0 <= step - 1 < G:
            stage_b(step - 1)
        if 0 <= step - 2 < G:
            stage_c(step - 2)
        if 0 <= step - 3 < G:
            if step == 3 and FLAG_Q:
                wait(qb, q_sem)
                if FLAG_COMPUTE:
                    for r in range(4):
                        qs[pl.ds(r * NQ, NQ), :] = qb[lax.rem(y - order(r) + 4, 4)]
            stage_d(step - 3)
            if FLAG_COMPUTE:
                compute(step - 3)
    if FLAG_COMPUTE:
        for r in range(4):
            rows = pl.ds(r * NQ, NQ)
            os[r] = (a_s[rows, :] / jnp.sum(l_s[rows, :], axis=1, keepdims=True)).astype(jnp.bfloat16)
        for dy in range(4):
            t = lax.rem(y - dy + 4, 4)
            ob[dy] = os[rank_ref[t]]
    if FLAG_O:
        for dy in range(4):
            send_o(dy)
        wait(out_ref, o_sem)
    else:
        out_ref[...] = q_ref[...]
    sent = k_ref.at[:, pl.ds(0, 31 * HS)]
    wait(sent, kv_send)
    wait(sent, kv_send)
    if FLAG_Q:
        wait(sent, q_send)
    if FLAG_O:
        wait(sent, o_send)
    for g in range(G):
        for right in (True, False):
            if FLAG_Y:
                y_copy(g, right).wait_send()
                far_copy(g, right).wait_send()
        if FLAG_D2D:
            for d in range(4):
                d2d_copy(g, d).wait_send()


def local(queries, keys, values, span_rank, token_counts):
    vmem = pl.BlockSpec(memory_space=pltpu.VMEM)
    smem = pl.BlockSpec(memory_space=pltpu.SMEM)
    dma = pltpu.SemaphoreType.DMA
    return pl.pallas_call(
        kernel,
        out_shape=jax.ShapeDtypeStruct(queries.shape, jnp.bfloat16),
        in_specs=[smem, smem, vmem, vmem, vmem],
        out_specs=vmem,
        scratch_shapes=[
            *[pltpu.VMEM((4, 2, KEYS, HS), jnp.bfloat16)] * G,
            pltpu.VMEM((4, NQ, HS), jnp.bfloat16),
            pltpu.VMEM((4 * NQ, HS), jnp.bfloat16),
            pltpu.VMEM((4, NQ, HS), jnp.bfloat16),
            pltpu.VMEM((4, NQ, HS), jnp.bfloat16),
            pltpu.VMEM((4 * NQ, HS), jnp.float32),
            pltpu.VMEM((4 * NQ, HS), jnp.float32),
            pltpu.VMEM((4 * NQ, HS), jnp.float32),
            dma((G,)), dma((G, 2)), dma((G, 2)), dma((G, 4)), dma, dma, dma, dma, dma, dma((G, 2)), dma((G, 2)), dma((G, 4)),
        ],
        compiler_params=pltpu.CompilerParams(has_side_effects=True, vmem_limit_bytes=48 * 2**20),
    )(span_rank, token_counts, queries, keys, values)


def solution(mesh):
    spec = P(("tm", "seq"), None)
    return jax.shard_map(
        local, mesh=mesh, in_specs=(spec, spec, spec, P(), P()), out_specs=spec, check_vma=False
    )
```

```python
import functools

import jax
import jax.numpy as jnp
from jax import lax
from jax.experimental import pallas as pl
from jax.experimental.pallas import tpu as pltpu
from jax.sharding import PartitionSpec as P

MESH = pl.DeviceIdType.MESH
HS = 128
NX, NZ, NY = 4, 8, 4
ROWS = 48
UNIT = NX * ROWS
HALF = 2 * UNIT
KEYS = 2 * HALF
NQ = 4 * ROWS
SCALE = HS ** (-0.5) * 1.4426950408889634
TK = 256
UNITS = (0, 1, 7, 2, 6, 4, 3, 5)
HALVES = {"n": (0, 1, 6, 7), "f": (4, 5, 2, 3)}
SENDS = (0, 1, 7, 2, 6, "n", "f", 4, 3, 5)
STEPS = (
    "a0", "a1", "a7", "a2", "a6", "b0", "b1", "b7", "b2", "b6", "f0", "f1",
    "qn", "qf", "c0b", "a4", "f7", "f2", "a3", "a5", "b4", "c1b", "b3", "b5",
    "f6", "f4", "c2b", "f3", "f5", "c3b", "of", "on",
)
PEERS = sorted(
    {(dx, dy, 0) for dx in range(NX) for dy in range(NY)}
    | {(dx, 0, dz) for dx in range(NX) for dz in range(NZ)}
    | {(dx, dz % NY, dz) for dx in range(NX) for dz in range(NZ)}
)


def far(offset):
    return sum(min(d, n - d) for d, n in zip(offset, (NX, NY, NZ)))


def lanesum(p):
    total = p[:, :HS]
    for at in range(HS, p.shape[1], HS):
        total = total + p[:, at : at + HS]
    return total


def kernel(rank_hbm, count_hbm, q_hbm, k_hbm, v_hbm, out_ref, kv0, kv1, kv2, kv3, q_ref, k_ref, v_ref,
           rank_ref, count_ref, qbn, qbf, qs, obn, obf, osn, osf, m_s, l_s, a_s,
           in_sem, a_sem, b_sem, f_sem, d_sem, q_sem, o_sem, kv_send, q_send, o_send, y_send, f_send, d_send):
    kvb = (kv0, kv1, kv2, kv3)
    qbs, obs, oss = {"n": qbn, "f": qbf}, {"n": obn, "f": obf}, {"n": osn, "f": osf}
    number = {"n": 0, "f": 1}
    y = lax.axis_index("tm")
    s = lax.axis_index("seq")
    h = s // 2
    c = s % 2
    x = h // NZ
    z = h % NZ

    def at(dx, dy, dz):
        hd = ((x + dx) % NX) * NZ + (z + dz) % NZ
        return (y + dy) % NY, hd

    def remote(src, dst, send, recv, where):
        return pltpu.make_async_remote_copy(src, dst, send, recv, device_id=where, device_id_type=MESH)

    def wait(ref, sem):
        pltpu.make_async_copy(ref, ref, sem).wait()

    def place(dz):
        n = UNITS.index(dz)
        return n // 2, (n % 2) * UNIT

    def mine(dz, spans):
        n, row = place(dz)
        return kvb[n].at[spans, :, pl.ds(row, UNIT), :]

    def theirs(dz, spans):
        n, row = place(dz)
        return kvb[n].at[spans, :, pl.ds(HALF + row, UNIT), :]

    ALL, OWN = pl.ds(0, 4), pl.ds(0, 1)

    def send_kv(dz):
        n, row = place(dz)
        for dy in (1, 3, 0) if dz == 0 else (0,):
            for dx in range(NX):
                yd, hd = at(dx, dy, dz)
                cols = pl.ds(pl.multiple_of(hd * HS, HS), HS)
                for j, ref in enumerate((k_ref, v_ref)):
                    src = ref.at[:, cols]
                    dst = kvb[n].at[(NY - dy) % NY, j, pl.ds(row + dx * ROWS, ROWS), :]
                    if (dx, dy, dz) == (0, 0, 0):
                        pltpu.make_async_copy(src, dst, a_sem.at[0]).start()
                    else:
                        recv = b_sem.at[0, dy] if dy else a_sem.at[dz]
                        remote(src, dst, kv_send, recv, (yd, 2 * hd + c)).start()

    def send_q(half):
        for dz in HALVES[half]:
            for dx in range(NX):
                dy = dz % NY
                yd, hd = at(dx, dy, dz)
                src = q_ref.at[:, pl.ds(pl.multiple_of(hd * HS, HS), HS)]
                dst = qbs[half].at[dy, pl.ds(dx * ROWS, ROWS), :]
                if (dx, dz) == (0, 0):
                    pltpu.make_async_copy(src, dst, q_sem.at[0]).start()
                else:
                    remote(src, dst, q_send, q_sem.at[number[half]], (yd, 2 * hd + c)).start()

    def sort_q(half):
        wait(qbs[half], q_sem.at[number[half]])
        for r in range(4):
            qs[pl.ds((2 * r + number[half]) * NQ, NQ), :] = qbs[half][lax.rem(y - order(r) + 4, 4)]

    def send_o(half):
        cols = pl.ds(pl.multiple_of(h * HS, HS), HS)
        for dz in HALVES[half]:
            for dx in range(NX):
                dy = dz % NY
                yd, hd = at(-dx, -dy, -dz)
                src = obs[half].at[dy, pl.ds(dx * ROWS, ROWS), :]
                dst = out_ref.at[:, cols]
                if (dx, dz) == (0, 0):
                    pltpu.make_async_copy(src, dst, o_sem).start()
                else:
                    remote(src, dst, o_send, o_sem, (yd, 2 * hd + c)).start()

    def finish(half):
        for r in range(4):
            rows = pl.ds((2 * r + number[half]) * NQ, NQ)
            total = jnp.sum(l_s[rows, :], axis=1, keepdims=True)
            oss[half][r] = (a_s[rows, :] / total).astype(jnp.bfloat16)
        for dy in range(NY):
            obs[half][dy] = oss[half][lax.rem(rank_ref[lax.rem(y - dy + 4, 4)], 4)]

    def y_copy(dz, dy):
        return remote(mine(dz, OWN), mine(dz, pl.ds(NY - dy, 1)), y_send.at[dz, dy], b_sem.at[dz, dy], ((y + dy) % NY, s))

    def f_copy(dz, dy):
        n, row = place(dz)
        j = 0 if dy == 1 else 1
        src = kvb[n].at[NY - dy, j, pl.ds(row, UNIT), :]
        dst = kvb[n].at[2, j, pl.ds(row, UNIT), :]
        return remote(src, dst, f_send.at[dz, dy], f_sem.at[dz], ((y + dy) % NY, s))

    def d_copy(dz, d):
        return remote(mine(dz, pl.ds(d, 1)), theirs(dz, pl.ds(d, 1)), d_send.at[dz, d], d_sem.at[dz], (y, s + 1 - 2 * c))

    def stage_a(dz):
        wait(mine(dz, OWN), a_sem.at[dz])
        if dz:
            for dy in (1, 3):
                y_copy(dz, dy).start()
        d_copy(dz, 0).start()

    def stage_b(dz):
        for dy in (1, 3):
            wait(mine(dz, pl.ds(NY - dy, 1)), b_sem.at[dz, dy])
            f_copy(dz, dy).start()
            d_copy(dz, NY - dy).start()

    def stage_f(dz):
        wait(mine(dz, pl.ds(2, 1)), f_sem.at[dz])
        d_copy(dz, 2).start()

    def order(r):
        return lax.rem(sum(jnp.where(rank_ref[t] == r, t, 0) for t in range(1, 4)), 4)

    def positions(n):
        col = lax.broadcasted_iota(jnp.int32, (8, KEYS), 1)
        pos = col
        for m in range(2):
            core = c if m == 0 else 1 - c
            for i, dz in enumerate(UNITS[2 * n : 2 * n + 2]):
                for dx in range(NX):
                    first = m * HALF + i * UNIT + dx * ROWS
                    _, hd = at(-dx, 0, -dz)
                    base = (2 * hd + core) * ROWS - first
                    pos = jnp.where((col >= first) & (col < first + ROWS), col + base, pos)
        return pos[:1]

    def compute(n, half):
        pos = positions(n)
        for j in range(4):
            t = order(j)
            d = lax.rem(t - y + 4, 4)
            limit = count_ref[t]
            if half == "b":
                pieces = [pl.ds(2 * j * NQ, (4 - j) * 2 * NQ)]
            else:
                pieces = [pl.ds((2 * r + number[half]) * NQ, NQ) for r in range(j, 4)]

            def get(ref):
                return jnp.concatenate([ref[rows, :] for rows in pieces], axis=0)

            def put(ref, new):
                first = 0
                for rows in pieces:
                    ref[rows, :] = new[first : first + rows.size]
                    first += rows.size

            queries = get(qs)
            for at_key in range(0, KEYS, TK):
                k = kvb[n][d, 0, at_key : at_key + TK, :]
                v = kvb[n][d, 1, at_key : at_key + TK, :]
                live = pos[:, at_key : at_key + TK] < limit
                scores = lax.dot_general(queries, k, (((1,), (1,)), ((), ())), preferred_element_type=jnp.float32)
                scores = jnp.where(live, scores, -1e30)
                before = get(m_s)
                upper = jnp.maximum(before, jnp.max(scores, axis=1, keepdims=True) * SCALE)
                rescale = jnp.exp2(before - upper)
                weights = jnp.exp2(scores * SCALE - jnp.concatenate([upper] * (TK // HS), axis=1))
                put(l_s, get(l_s) * rescale + lanesum(weights))
                put(a_s, get(a_s) * rescale + jnp.dot(
                    weights.astype(jnp.bfloat16), v, preferred_element_type=jnp.float32))
                put(m_s, upper)

    ready = set()

    def run_step(step):
        kind, what = step[0], step[1:]
        if kind == "a":
            stage_a(int(what))
        elif kind == "b":
            stage_b(int(what))
        elif kind == "f":
            stage_f(int(what))
        elif kind == "q":
            sort_q(what)
        elif kind == "c":
            n = int(what[0])
            if n not in ready:
                for dz in UNITS[2 * n : 2 * n + 2]:
                    wait(theirs(dz, ALL), d_sem.at[dz])
            ready.add(n)
            compute(n, what[1])
        elif kind == "o":
            finish(what)
            send_o(what)

    barrier = pltpu.get_barrier_semaphore()
    for dx, dy, dz in sorted(PEERS, key=far, reverse=True):
        if (dx, dy, dz) != (0, 0, 0):
            yd, hd = at(dx, dy, dz)
            pl.semaphore_signal(barrier, inc=1, device_id=(yd, 2 * hd + c), device_id_type=MESH)
    pl.semaphore_signal(barrier, inc=1, device_id=(y, s + 1 - 2 * c), device_id_type=MESH)
    loads = [
        pltpu.make_async_copy(src, dst, in_sem.at[i])
        for i, (src, dst) in enumerate(
            ((k_hbm, k_ref), (v_hbm, v_ref), (q_hbm, q_ref), (rank_hbm, rank_ref), (count_hbm, count_ref))
        )
    ]
    for load in loads:
        load.start()
    for load in loads:
        load.wait()
    pl.semaphore_wait(barrier, len(PEERS))

    for what in SENDS:
        if what in HALVES:
            send_q(what)
        else:
            send_kv(what)
    m_s[...] = jnp.full(m_s.shape, -1e30, jnp.float32)
    l_s[...] = jnp.zeros(l_s.shape, jnp.float32)
    a_s[...] = jnp.zeros(a_s.shape, jnp.float32)
    for step in STEPS:
        run_step(step)
    wait(out_ref, o_sem)
    sent = k_ref.at[:, pl.ds(0, 31 * HS)]
    for _ in range(2):
        wait(sent, kv_send)
        wait(k_ref.at[:, pl.ds(0, 8 * HS)], kv_send)
    wait(sent, q_send)
    wait(sent, o_send)
    for dz in UNITS:
        for dy in (1, 3):
            if dz:
                y_copy(dz, dy).wait_send()
            f_copy(dz, dy).wait_send()
        for d in range(NY):
            d_copy(dz, d).wait_send()


def local(queries, keys, values, span_rank, token_counts):
    vmem = pl.BlockSpec(memory_space=pltpu.VMEM)
    hbm = pl.BlockSpec(memory_space=pltpu.HBM)
    dma = pltpu.SemaphoreType.DMA
    shape = queries.shape
    return pl.pallas_call(
        kernel,
        out_shape=jax.ShapeDtypeStruct(shape, jnp.bfloat16),
        in_specs=[hbm] * 5,
        out_specs=vmem,
        scratch_shapes=[
            *[pltpu.VMEM((4, 2, KEYS, HS), jnp.bfloat16)] * 4,
            *[pltpu.VMEM(shape, jnp.bfloat16)] * 3,
            pltpu.SMEM((4,), jnp.int32),
            pltpu.SMEM((4,), jnp.int32),
            *[pltpu.VMEM((4, NQ, HS), jnp.bfloat16)] * 2,
            pltpu.VMEM((8 * NQ, HS), jnp.bfloat16),
            *[pltpu.VMEM((4, NQ, HS), jnp.bfloat16)] * 4,
            *[pltpu.VMEM((8 * NQ, HS), jnp.float32)] * 3,
            dma((5,)), dma((8,)), dma((8, 4)), dma((8,)), dma((8,)), dma((2,)), dma, dma, dma, dma, dma((8, 4)), dma((8, 4)), dma((8, 4)),
        ],
        compiler_params=pltpu.CompilerParams(
            has_side_effects=True, collective_id=0, vmem_limit_bytes=48 * 2**20
        ),
    )(span_rank, token_counts, queries, keys, values)


def solution(mesh):
    spec = P(("tm", "seq"), None)
    return jax.shard_map(
        local, mesh=mesh, in_specs=(spec, spec, spec, P(), P()), out_specs=spec, check_vma=False
    )
```
